256 devices in a mesh: inp: 16 (over z, core), out: 16 (over x, y).
Axes of the slice: x: 4, y: 4, z: 8, core: 2. Of those that a mesh axis runs over, the one named last changes fastest.
Arguments:
- phases: bfloat16 [1024, 32768], P(None, 'inp'), may hold values from -3.140625 to 3.140625
- transfer_re: bfloat16 [32768, 4096], P('inp', 'out'), may hold values from -16 to 16
- transfer_im: bfloat16 [32768, 4096], P('inp', 'out'), may hold values from -16 to 16
- measured: float32 [1024, 4096], P(None, 'out'), may hold values from 0.1 to 4
Outputs:
- grad_re: float32 [32768, 4096], P('inp', 'out')
- grad_im: float32 [32768, 4096], P('inp', 'out')
The draws below stay inside these ranges and needn't reach their ends.
All inputs are finite; a program needn't handle non-finite values.
Results may differ from the reference program's by a relative error of at most 0.0049.
Values may be sent and summed in bfloat16 or wider, within the bound.
A program may use at most 64 MiB of HBM per device.

```python
import math
import jax
import jax.numpy as jnp
from jax import lax

NIN = 32768
NOUT = 4096
P_SIZE = 1024


def column_envelope(key, reach):
    key = jax.random.fold_in(key, 101)
    ramp = 1.0 + 2.0 * jnp.arange(NOUT, dtype=jnp.float32) / max(NOUT - 1, 1)
    spread = jnp.exp(jax.random.uniform(key, (NOUT,), jnp.float32) * reach)
    return ramp * spread / 3.0


def draw_entries(key, envelope):
    values = jax.random.normal(key, (NIN, NOUT), jnp.float32)
    return values * (0.70710678 / jnp.sqrt(jnp.float32(NIN))) * envelope[None, :]


def draw_transfer_re(key, part):
    envelope = column_envelope(key, 1.0986123)
    key = jax.random.fold_in(key, 1)
    return draw_entries(key, envelope).astype(jnp.bfloat16)


def draw_transfer_im(key, part):
    envelope = column_envelope(key, 1.0986123)
    key = jax.random.fold_in(key, 2)
    return draw_entries(key, envelope).astype(jnp.bfloat16)


def level_of(stream_key, extent, pieces, smallest, largest):
    factor_of, own = 1.0, jax.random.fold_in(stream_key, 6)
    for dim, parts in pieces:
        steps = jnp.exp(jax.random.uniform(jax.random.fold_in(own, dim), (parts,), jnp.float32, smallest / len(pieces), largest / len(pieces)))
        factor_of = factor_of * jnp.repeat(steps, extent[dim] // parts).reshape([-1 if axis == dim else 1 for axis in range(len(extent))])
    return factor_of


def setup_inputs(seed: int = 0) -> dict:
    key_of = jax.random.split(jax.random.key(seed), 5)
    return {
        "phases": jnp.clip(jax.random.uniform(key_of[0], (P_SIZE, NIN), jnp.float32, -3.140625, 3.140625), -3.140625, 3.140625).astype(jnp.bfloat16),
        "transfer_re": draw_transfer_re(jax.random.fold_in(key_of[4], 71), 0),
        "transfer_im": draw_transfer_im(jax.random.fold_in(key_of[4], 71), 0),
        "measured": jnp.clip(jnp.exp(math.log(4.0) - 3.6888794 * jax.random.uniform(key_of[3], (P_SIZE, NOUT), jnp.float32) ** level_of(key_of[3], (P_SIZE, NOUT), ((1, 16),), -0.2, 0.2)), 0.1, 4.0),
    }


def reference(phases, transfer_re, transfer_im, measured):
    angle = phases.astype(jnp.float32)
    probe_re = jnp.cos(angle).astype(jnp.bfloat16)
    probe_im = jnp.sin(angle).astype(jnp.bfloat16)
    field_re = jnp.dot(probe_re, transfer_re, preferred_element_type=jnp.float32) - jnp.dot(probe_im, transfer_im, preferred_element_type=jnp.float32)
    field_im = jnp.dot(probe_re, transfer_im, preferred_element_type=jnp.float32) + jnp.dot(probe_im, transfer_re, preferred_element_type=jnp.float32)
    power = field_re * field_re + field_im * field_im
    scale = lax.optimization_barrier(jnp.sum(measured, axis=1)) / (lax.optimization_barrier(jnp.sum(power, axis=1)) + 1e-05)
    misfit = scale[:, None] * power - measured
    factor = scale[:, None] * misfit
    weight_re = (factor * field_re).astype(jnp.bfloat16)
    weight_im = (factor * field_im).astype(jnp.bfloat16)
    contract = (((0,), (0,)), ((), ()))
    norm = 1.0 / jnp.sqrt(jnp.float32(P_SIZE))
    grad_re = (lax.dot_general(probe_re, weight_re, contract, preferred_element_type=jnp.float32) + lax.dot_general(probe_im, weight_im, contract, preferred_element_type=jnp.float32)) * norm
    grad_im = (lax.dot_general(probe_re, weight_im, contract, preferred_element_type=jnp.float32) - lax.dot_general(probe_im, weight_re, contract, preferred_element_type=jnp.float32)) * norm
    return (grad_re, grad_im)
```

```python
import functools

import jax
import jax.numpy as jnp
from jax import lax
from jax.experimental import pallas as pl
from jax.experimental.pallas import tpu as pltpu
from jax.sharding import PartitionSpec as P

P_SIZE = 1024
MESH = pl.DeviceIdType.MESH
F32 = jnp.float32
BF16 = jnp.bfloat16
SIN = (7.07104388e-01, -2.94595328e-02, 3.67091170e-04, -2.02891555e-06)
COS = (1.41421350e00, -1.76776361e-01, 3.68257540e-03, -3.06126501e-05, 1.27908569e-07)


def cos_sin(x):
    u = x * x
    s = x * (SIN[0] + u * (SIN[1] + u * (SIN[2] + u * SIN[3])))
    c = COS[0] + u * (COS[1] + u * (COS[2] + u * (COS[3] + u * COS[4])))
    return 1.0 - s * s, s * c


def twice(w, n):
    return jnp.concatenate([w, jnp.concatenate([w[:, n:], -w[:, :n]], axis=1)], axis=0)


def front(
    zs, outs, ph_hbm, tr_hbm, ti_hbm, me_hbm, acc_hbm, pt_hbm, w_hbm,
    ph, rhs, meas, pt, acc, part, give, sib, ring, send, field, pw, pws, w,
    in_sem, t_sem, o_sem, sib_s, sib_r, ring_s, ring_r, pw_s, pw_r,
    agl_s, agl_r, ags_s, ags_r, agb_s, agb_r,
):
    chunk, half, n = ph.shape[1], ph.shape[1] // 2, meas.shape[1]
    depth, slab = ph.shape[2], min(256, ph.shape[2])
    sub = half // 2
    me = lax.axis_index("inp")
    peer = lax.axis_index("out")
    z, core = me // 2, me % 2
    step = 1 - 2 * core
    ahead = lax.rem(z + step + zs, zs) * 2 + core
    behind = lax.rem(z - step + zs, zs) * 2 + core
    other = z * 2 + 1 - core
    mine = pl.multiple_of(core * half, half)
    theirs = pl.multiple_of((1 - core) * half, half)

    def chunk_of(i):
        off = jnp.where(i % 2 == 1, 4 - (i + 1) // 2, i // 2 - 4)
        return lax.rem(z + off + zs, zs)

    def load_phase(i):
        rows = pl.ds(pl.multiple_of(chunk_of(i) * chunk, chunk), chunk)
        return pltpu.make_async_copy(ph_hbm.at[rows], ph.at[i], in_sem.at[i])

    loads = [
        pltpu.make_async_copy(tr_hbm, rhs.at[0, :, pl.ds(0, n)], t_sem.at[0]),
        pltpu.make_async_copy(ti_hbm, rhs.at[0, :, pl.ds(n, n)], t_sem.at[1]),
        pltpu.make_async_copy(tr_hbm, rhs.at[1, :, pl.ds(n, n)], t_sem.at[2]),
    ]
    load_phase(0).start()
    for copy in loads:
        copy.start()
    for i in range(1, zs):
        load_phase(i).start()
    own_rows = pl.ds(pl.multiple_of(z * chunk + core * half, half), half)
    load_meas = pltpu.make_async_copy(me_hbm.at[own_rows], meas, t_sem.at[3])
    load_meas.start()

    barrier = pltpu.get_barrier_semaphore()
    for target in (other, ahead, behind):
        pl.semaphore_signal(barrier, inc=1, device_id={"inp": target}, device_id_type=MESH)
    for j in range(1, outs):
        pl.semaphore_signal(
            barrier, inc=1, device_id={"out": lax.rem(peer + j, outs)}, device_id_type=MESH
        )

    for copy in loads:
        copy.wait()
    rhs[1, :, 0:n] = -rhs[0, :, n:]

    def to_sibling(i):
        return pltpu.make_async_remote_copy(
            src_ref=give.at[i], dst_ref=sib.at[i], send_sem=sib_s.at[i], recv_sem=sib_r.at[i],
            device_id={"inp": other}, device_id_type=MESH,
        )

    def round_ring(e, h):
        target = jnp.where(e % 2 == 0, ahead, behind)
        rows = pl.ds(h * sub, sub)
        return pltpu.make_async_remote_copy(
            src_ref=send.at[e, rows], dst_ref=ring.at[e, rows],
            send_sem=ring_s.at[e, h], recv_sem=ring_r.at[e, h],
            device_id={"inp": target}, device_id_type=MESH,
        )

    def forward(i):
        load_phase(i).wait()
        total = None
        for j in range(depth // slab):
            cols = slice(j * slab, (j + 1) * slab)
            re, im = cos_sin(ph[i, :, cols].astype(F32))
            re, im = re.astype(BF16), im.astype(BF16)
            pt[i, cols, 0:chunk] = re.T
            pt[i, cols, chunk:] = im.T
            left = jnp.concatenate([re, im], axis=1)
            right = jnp.concatenate([rhs[0, cols, :], rhs[1, cols, :]], axis=0)
            term = jnp.dot(left, right, preferred_element_type=F32)
            total = term if total is None else total + term
        field[...] = total
        part[i] = field[pl.ds(mine, half), :]
        give[i] = field[pl.ds(theirs, half), :]

    def event(e):
        swap = jnp.where((e >= 1) & (e <= 6), jnp.where(e % 2 == 1, 1, -1), 0)
        i = e + swap * (1 - core)
        to_sibling(i).wait_recv()
        for h in range(2):
            rows = slice(h * sub, (h + 1) * sub)
            value = part[i, rows, :] + sib[i, rows, :]

            @pl.when(e < 2)
            def _():
                send[e, rows, :] = value

            @pl.when(e >= 2)
            def _():
                round_ring(e - 2, h).wait_recv()
                send[e, rows, :] = value + ring[e - 2, rows, :]

            round_ring(e, h).start()

    def body(i, _):
        forward(i)

        @pl.when(i == 0)
        def _():
            pl.semaphore_wait(barrier, 3 + outs - 1)

        to_sibling(i).start()

        @pl.when(i >= 1)
        def _():
            event(i - 1)

        return 0

    lax.fori_loop(0, zs, body, 0)

    load_meas.wait()
    light = meas[...]
    to_sibling(zs - 1).wait_recv()
    total = part[zs - 1] + sib[zs - 1]
    for h in range(2):
        round_ring(zs - 3, h).wait_recv()
    total = total + ring[zs - 3]
    for h in range(2):
        round_ring(zs - 2, h).wait_recv()
    total = total + ring[zs - 2]
    f_re, f_im = total[:, :n], total[:, n:]
    power = f_re * f_re + f_im * f_im

    def lane_sum(v):
        folded = v[:, 0:128]
        for k in range(1, n // 128):
            folded = folded + v[:, k * 128 : (k + 1) * 128]
        return jnp.sum(folded.T, axis=0, keepdims=True)

    pws[...] = jnp.concatenate(
        [lane_sum(power), lane_sum(light), jnp.zeros((6, half), F32)], axis=0
    )

    def to_peer(j):
        return pltpu.make_async_remote_copy(
            src_ref=pws, dst_ref=pw.at[j], send_sem=pw_s.at[j], recv_sem=pw_r.at[j],
            device_id={"out": lax.rem(peer + j, outs)}, device_id_type=MESH,
        )

    for j in range(1, outs):
        to_peer(j).start()
    sums = pws[...]
    for j in range(1, outs):
        to_peer(j).wait_recv()
        sums = sums + pw[j]
    scale = sums[1:2, :] / (sums[0:1, :] + 1e-05)
    scale = jnp.broadcast_to(scale, (128, half)).T
    scale = jnp.concatenate([scale] * (n // 128), axis=1)
    factor = scale * (scale * power - light)
    own = pl.ds(mine, half)
    w[zs - 1, own, 0:n] = (factor * f_re).astype(BF16)
    w[zs - 1, own, n:] = (factor * f_im).astype(BF16)

    def long_slot(t):
        return zs - 1 if t == 0 else 8 - 2 * t - (core if t < 4 else 0)

    def short_slot(t):
        return zs - 1 if t == 0 else 7 - 2 * t + core

    def pass_on(slot_of, sems, target, t, h):
        rows = pl.ds(pl.multiple_of(mine + h * sub, sub), sub)
        slot = slot_of(t)
        there = slot_of(t + 1)
        return pltpu.make_async_remote_copy(
            src_ref=w.at[slot, rows], dst_ref=w.at[there, rows],
            send_sem=sems[0].at[t, h], recv_sem=sems[1].at[t, h],
            device_id={"inp": target}, device_id_type=MESH,
        )

    def go_long(t, h):
        return pass_on(long_slot, (agl_s, agl_r), ahead, t, h)

    def go_short(t, h):
        return pass_on(short_slot, (ags_s, ags_r), behind, t, h)

    def share(slot, h, rows0):
        rows = pl.ds(pl.multiple_of(rows0 + h * sub, sub), sub)
        return pltpu.make_async_remote_copy(
            src_ref=w.at[slot, rows], dst_ref=w.at[slot, rows],
            send_sem=agb_s.at[slot, h], recv_sem=agb_r.at[slot, h],
            device_id={"inp": other}, device_id_type=MESH,
        )

    for h in range(2):
        go_long(0, h).start()
        go_short(0, h).start()
    for h in range(2):
        share(zs - 1, h, mine).start()

    block = min(256, depth)

    def backward(slots, first):
        def rows_of(b, _):
            rows = pl.ds(pl.multiple_of(b * block, block), block)
            value = None
            for s in slots:
                term = jnp.dot(pt[s, rows, :], twice(w[s], n), preferred_element_type=F32)
                value = term if value is None else value + term
            if not first:
                value = value + acc[rows, :]
            acc[rows, :] = value
            return 0

        lax.fori_loop(0, depth // block, rows_of, 0)

    for t in range(1, 5):
        for h in range(2):
            go_long(t - 1, h).wait_recv()
            if t < 4:
                go_long(t, h).start()
            share(long_slot(t), h, mine).start()
            if t < 4:
                go_short(t - 1, h).wait_recv()
                if t < 3:
                    go_short(t, h).start()
                share(short_slot(t), h, mine).start()
        slots = (zs - 1,) if t == 1 else (9 - 2 * t, 10 - 2 * t)
        for s in slots:
            for h in range(2):
                share(s, h, theirs).wait_recv()
        backward(slots, t == 1)

    out_acc = pltpu.make_async_copy(acc, acc_hbm, o_sem.at[0])
    out_acc.start()
    out_pt = pltpu.make_async_copy(pt.at[0], pt_hbm, o_sem.at[1])
    out_pt.start()
    for h in range(2):
        share(0, h, theirs).wait_recv()
    out_w = pltpu.make_async_copy(w.at[0], w_hbm, o_sem.at[2])
    out_w.start()

    def drain(i, _):
        to_sibling(i).wait_send()
        for h in range(2):
            share(i, h, mine).wait_send()
        return 0

    lax.fori_loop(0, zs, drain, 0)

    def drain_ring(e, _):
        for h in range(2):
            round_ring(e, h).wait_send()
        return 0

    lax.fori_loop(0, zs - 1, drain_ring, 0)
    for j in range(1, outs):
        to_peer(j).wait_send()
    for h in range(2):
        for t in range(4):
            go_long(t, h).wait_send()
        for t in range(3):
            go_short(t, h).wait_send()
    out_acc.wait()
    out_pt.wait()
    out_w.wait()


def finish(acc, pt, w, re, im):
    n = re.shape[1]
    value = acc[...] + jnp.dot(pt[...], twice(w[...], n), preferred_element_type=F32)
    norm = 1.0 / float(P_SIZE) ** 0.5
    re[...] = value[:, :n] * norm
    im[...] = value[:, n:] * norm


def body(zs, outs, phases, transfer_re, transfer_im, measured):
    probes, depth = phases.shape
    n = transfer_re.shape[1]
    chunk = probes // zs
    half = chunk // 2
    DMA = pltpu.SemaphoreType.DMA
    anywhere = pl.BlockSpec(memory_space=pl.ANY)
    acc, pt, w = pl.pallas_call(
        functools.partial(front, zs, outs),
        out_shape=(
            jax.ShapeDtypeStruct((depth, 2 * n), F32),
            jax.ShapeDtypeStruct((depth, 2 * chunk), BF16),
            jax.ShapeDtypeStruct((chunk, 2 * n), BF16),
        ),
        in_specs=[anywhere] * 4,
        out_specs=(anywhere,) * 3,
        scratch_shapes=[
            pltpu.VMEM((zs, chunk, depth), BF16),
            pltpu.VMEM((2, depth, 2 * n), BF16),
            pltpu.VMEM((half, n), F32),
            pltpu.VMEM((zs, depth, 2 * chunk), BF16),
            pltpu.VMEM((depth, 2 * n), F32),
            pltpu.VMEM((zs, half, 2 * n), F32),
            pltpu.VMEM((zs, half, 2 * n), F32),
            pltpu.VMEM((zs, half, 2 * n), F32),
            pltpu.VMEM((zs - 1, half, 2 * n), F32),
            pltpu.VMEM((zs - 1, half, 2 * n), F32),
            pltpu.VMEM((chunk, 2 * n), F32),
            pltpu.VMEM((outs, 8, half), F32),
            pltpu.VMEM((8, half), F32),
            pltpu.VMEM((zs, chunk, 2 * n), BF16),
            DMA((zs,)), DMA((4,)), DMA((3,)),
            DMA((zs,)), DMA((zs,)),
            DMA((zs - 1, 2)), DMA((zs - 1, 2)),
            DMA((outs,)), DMA((outs,)),
            DMA((4, 2)), DMA((4, 2)), DMA((3, 2)), DMA((3, 2)),
            DMA((zs, 2)), DMA((zs, 2)),
        ],
        compiler_params=pltpu.CompilerParams(
            collective_id=0, has_side_effects=True, vmem_limit_bytes=50 * 1024 * 1024
        ),
    )(phases, transfer_re, transfer_im, measured)
    block = min(512, depth)
    return pl.pallas_call(
        finish,
        grid=(depth // block,),
        out_shape=(jax.ShapeDtypeStruct((depth, n), F32),) * 2,
        in_specs=[
            pl.BlockSpec((block, 2 * n), lambda b: (b, 0)),
            pl.BlockSpec((block, 2 * chunk), lambda b: (b, 0)),
            pl.BlockSpec((chunk, 2 * n), lambda b: (0, 0)),
        ],
        out_specs=(pl.BlockSpec((block, n), lambda b: (b, 0)),) * 2,
    )(acc, pt, w)


def solution(mesh):
    in_specs = (P(None, "inp"), P("inp", "out"), P("inp", "out"), P(None, "out"))
    out_specs = (P("inp", "out"), P("inp", "out"))
    fn = functools.partial(body, mesh.shape["inp"] // 2, mesh.shape["out"])
    return jax.shard_map(fn, mesh=mesh, in_specs=in_specs, out_specs=out_specs, check_vma=False)
```

```python
import functools

import jax
import jax.numpy as jnp
from jax import lax
from jax.experimental import pallas as pl
from jax.experimental.pallas import tpu as pltpu
from jax.sharding import PartitionSpec as P

P_SIZE = 1024
MESH = pl.DeviceIdType.MESH
TREE = ((0, 2), (0, -2), (0, 1), (0, -1), (2, 4), (2, 3), (-2, -3))
LATE = 3
PIECES = 4
F32 = jnp.float32
BF16 = jnp.bfloat16
SIN = (7.07104388e-01, -2.94595328e-02, 3.67091170e-04, -2.02891555e-06)
COS = (1.41421350e00, -1.76776361e-01, 3.68257540e-03, -3.06126501e-05, 1.27908569e-07)


def cos_sin(x):
    u = x * x
    s = x * (SIN[0] + u * (SIN[1] + u * (SIN[2] + u * SIN[3])))
    c = COS[0] + u * (COS[1] + u * (COS[2] + u * (COS[3] + u * COS[4])))
    return 1.0 - s * s, s * c


def twice(w, n):
    return jnp.concatenate([w, jnp.concatenate([w[:, n:], -w[:, :n]], axis=1)], axis=0)


def front(
    zs, outs, ph_hbm, tr_hbm, ti_hbm, me_hbm, acc, pt, w_late,
    ph, rhs, meas, part, give, sib, ring, send, field, pw, pws, w,
    in_sem, t_sem, sib_s, sib_r, ring_s, ring_r, pw_s, pw_r, ag_s, ag_r, agb_s, agb_r,
):
    chunk, half, n = ph.shape[1], ph.shape[1] // 2, meas.shape[1]
    depth, slab = ph.shape[2], min(256, ph.shape[2])
    sub = half // 2
    me = lax.axis_index("inp")
    peer = lax.axis_index("out")
    z, core = me // 2, me % 2
    step = 1 - 2 * core

    def at(d):
        return lax.rem(z + step * d + zs, zs) * 2 + core

    ahead, behind = at(1), at(-1)
    other = z * 2 + 1 - core
    mine = pl.multiple_of(core * half, half)
    theirs = pl.multiple_of((1 - core) * half, half)

    def chunk_of(i):
        off = jnp.where(i % 2 == 1, 4 - (i + 1) // 2, i // 2 - 4)
        return lax.rem(z + off + zs, zs)

    def load_phase(i):
        rows = pl.ds(pl.multiple_of(chunk_of(i) * chunk, chunk), chunk)
        return pltpu.make_async_copy(ph_hbm.at[rows], ph.at[i], in_sem.at[i])

    loads = [
        pltpu.make_async_copy(tr_hbm, rhs.at[0, :, pl.ds(0, n)], t_sem.at[0]),
        pltpu.make_async_copy(ti_hbm, rhs.at[0, :, pl.ds(n, n)], t_sem.at[1]),
        pltpu.make_async_copy(tr_hbm, rhs.at[1, :, pl.ds(n, n)], t_sem.at[2]),
    ]
    load_phase(0).start()
    for copy in loads:
        copy.start()
    for i in range(1, zs):
        load_phase(i).start()
    own_rows = pl.ds(pl.multiple_of(z * chunk + core * half, half), half)
    load_meas = pltpu.make_async_copy(me_hbm.at[own_rows], meas, t_sem.at[3])
    load_meas.start()

    barrier = pltpu.get_barrier_semaphore()
    for target in (other, ahead, behind, at(2), at(-2)):
        pl.semaphore_signal(barrier, inc=1, device_id={"inp": target}, device_id_type=MESH)
    for j in range(1, outs):
        pl.semaphore_signal(
            barrier, inc=1, device_id={"out": lax.rem(peer + j, outs)}, device_id_type=MESH
        )

    for copy in loads:
        copy.wait()
    rhs[1, :, 0:n] = -rhs[0, :, n:]

    def to_sibling(i):
        return pltpu.make_async_remote_copy(
            src_ref=give.at[i], dst_ref=sib.at[i], send_sem=sib_s.at[i], recv_sem=sib_r.at[i],
            device_id={"inp": other}, device_id_type=MESH,
        )

    def round_ring(e, h):
        target = jnp.where(e % 2 == 0, ahead, behind)
        rows = pl.ds(h * sub, sub)
        return pltpu.make_async_remote_copy(
            src_ref=send.at[e, rows], dst_ref=ring.at[e, rows],
            send_sem=ring_s.at[e, h], recv_sem=ring_r.at[e, h],
            device_id={"inp": target}, device_id_type=MESH,
        )

    def forward(i):
        load_phase(i).wait()
        total = None
        for j in range(depth // slab):
            cols = slice(j * slab, (j + 1) * slab)
            re, im = cos_sin(ph[i, :, cols].astype(F32))
            re, im = re.astype(BF16), im.astype(BF16)
            pt[i, cols, 0:chunk] = re.T
            pt[i, cols, chunk:] = im.T
            left = jnp.concatenate([re, im], axis=1)
            right = jnp.concatenate([rhs[0, cols, :], rhs[1, cols, :]], axis=0)
            term = jnp.dot(left, right, preferred_element_type=F32)
            total = term if total is None else total + term
        field[...] = total
        part[i] = field[pl.ds(mine, half), :]
        give[i] = field[pl.ds(theirs, half), :]

    def event(e):
        swap = jnp.where((e >= 1) & (e <= 6), jnp.where(e % 2 == 1, 1, -1), 0)
        i = e + swap * (1 - core)
        to_sibling(i).wait_recv()
        for h in range(2):
            rows = slice(h * sub, (h + 1) * sub)
            value = part[i, rows, :] + sib[i, rows, :]

            @pl.when(e < 2)
            def _():
                send[e, rows, :] = value

            @pl.when(e >= 2)
            def _():
                round_ring(e - 2, h).wait_recv()
                send[e, rows, :] = value + ring[e - 2, rows, :]

            round_ring(e, h).start()

    def body(i, _):
        forward(i)

        @pl.when(i == 0)
        def _():
            pl.semaphore_wait(barrier, 5 + outs - 1)

        to_sibling(i).start()

        @pl.when(i >= 1)
        def _():
            event(i - 1)

        return 0

    lax.fori_loop(0, zs, body, 0)

    load_meas.wait()
    light = meas[...]
    to_sibling(zs - 1).wait_recv()
    total = part[zs - 1] + sib[zs - 1]
    for h in range(2):
        round_ring(zs - 3, h).wait_recv()
    total = total + ring[zs - 3]
    for h in range(2):
        round_ring(zs - 2, h).wait_recv()
    total = total + ring[zs - 2]
    f_re, f_im = total[:, :n], total[:, n:]
    power = f_re * f_re + f_im * f_im

    def lane_sum(v):
        folded = v[:, 0:128]
        for k in range(1, n // 128):
            folded = folded + v[:, k * 128 : (k + 1) * 128]
        return jnp.sum(folded.T, axis=0, keepdims=True)

    pws[...] = jnp.concatenate(
        [lane_sum(power), lane_sum(light), jnp.zeros((6, half), F32)], axis=0
    )

    def to_peer(j):
        return pltpu.make_async_remote_copy(
            src_ref=pws, dst_ref=pw.at[j], send_sem=pw_s.at[j], recv_sem=pw_r.at[j],
            device_id={"out": lax.rem(peer + j, outs)}, device_id_type=MESH,
        )

    for j in range(1, outs):
        to_peer(j).start()
    sums = pws[...]
    for j in range(1, outs):
        to_peer(j).wait_recv()
        sums = sums + pw[j]
    scale = sums[1:2, :] / (sums[0:1, :] + 1e-05)
    scale = jnp.broadcast_to(scale, (128, half)).T
    scale = jnp.concatenate([scale] * (n // 128), axis=1)
    factor = scale * (scale * power - light)
    own = pl.ds(mine, half)
    w[zs - 1, own, 0:n] = (factor * f_re).astype(BF16)
    w[zs - 1, own, n:] = (factor * f_im).astype(BF16)

    def slot_of(d):
        if d == 0:
            return zs - 1
        if d == 4:
            return 0
        return 8 - 2 * d - core if d > 0 else 7 + 2 * d + core

    def pass_on(k):
        d, there = TREE[k]
        rows = pl.ds(mine, half)
        return pltpu.make_async_remote_copy(
            src_ref=w.at[slot_of(d), rows], dst_ref=w.at[slot_of(there), rows],
            send_sem=ag_s.at[k], recv_sem=ag_r.at[k],
            device_id={"inp": at(there - d)}, device_id_type=MESH,
        )

    def share(slot, rows0):
        rows = pl.ds(rows0, half)
        return pltpu.make_async_remote_copy(
            src_ref=w.at[slot, rows], dst_ref=w.at[slot, rows],
            send_sem=agb_s.at[slot], recv_sem=agb_r.at[slot],
            device_id={"inp": other}, device_id_type=MESH,
        )

    def arrive(k):
        pass_on(k).wait_recv()
        for later in range(len(TREE)):
            if TREE[later][0] == TREE[k][1]:
                pass_on(later).start()
        share(slot_of(TREE[k][1]), mine).start()

    block = min(512, depth)

    def backward(slots, first):
        for s in slots:
            share(s, theirs).wait_recv()

        def rows_of(b, _):
            rows = pl.ds(pl.multiple_of(b * block, block), block)
            value = None
            for s in slots:
                term = jnp.dot(pt[s, rows, :], twice(w[s], n), preferred_element_type=F32)
                value = term if value is None else value + term
            if not first:
                value = value + acc[rows, :]
            acc[rows, :] = value
            return 0

        lax.fori_loop(0, depth // block, rows_of, 0)

    for k in range(4):
        pass_on(k).start()
    share(zs - 1, mine).start()
    backward((zs - 1,), True)
    for k in (0, 1, 2, 3):
        arrive(k)
    backward((3, 4, 5, 6), False)
    for k in (6, 5, 4):
        arrive(k)
    for s in range(LATE):
        share(s, theirs).wait_recv()
        w_late[s] = w[s]

    def drain(i, _):
        to_sibling(i).wait_send()
        share(i, mine).wait_send()
        return 0

    lax.fori_loop(0, zs, drain, 0)

    def drain_ring(e, _):
        for h in range(2):
            round_ring(e, h).wait_send()
        return 0

    lax.fori_loop(0, zs - 1, drain_ring, 0)
    for j in range(1, outs):
        to_peer(j).wait_send()
    for k in range(len(TREE)):
        pass_on(k).wait_send()


def finish(acc, pt, w, re_hbm, im_hbm, re, im, sem):
    n, depth = re.shape[1], re.shape[0]
    block = depth // PIECES
    norm = 1.0 / float(P_SIZE) ** 0.5
    copies = []
    for b in range(PIECES):
        rows = slice(b * block, (b + 1) * block)
        value = acc[rows, :]
        for s in range(LATE):
            value = value + jnp.dot(pt[s, rows, :], twice(w[s], n), preferred_element_type=F32)
        re[rows, :] = value[:, :n] * norm
        im[rows, :] = value[:, n:] * norm
        for i, (here, there) in enumerate(((re, re_hbm), (im, im_hbm))):
            there = there.at[pl.ds(b * block, block)]
            copies.append(pltpu.make_async_copy(here.at[pl.ds(b * block, block)], there, sem.at[b, i]))
            copies[-1].start()
    for copy in copies:
        copy.wait()


def body(zs, outs, phases, transfer_re, transfer_im, measured):
    probes, depth = phases.shape
    n = transfer_re.shape[1]
    chunk = probes // zs
    half = chunk // 2
    DMA = pltpu.SemaphoreType.DMA
    anywhere = pl.BlockSpec(memory_space=pl.ANY)
    near = pl.BlockSpec(memory_space=pltpu.VMEM)
    operands = [
        pltpu.with_memory_space_constraint(v, pltpu.HBM)
        for v in (phases, transfer_re, transfer_im, measured)
    ]
    acc, pt, w = pl.pallas_call(
        functools.partial(front, zs, outs),
        out_shape=(
            pltpu.VMEM((depth, 2 * n), F32),
            pltpu.VMEM((zs, depth, 2 * chunk), BF16),
            pltpu.VMEM((LATE, chunk, 2 * n), BF16),
        ),
        in_specs=[pl.BlockSpec(memory_space=pltpu.HBM)] * 4,
        out_specs=(near,) * 3,
        scratch_shapes=[
            pltpu.VMEM((zs, chunk, depth), BF16),
            pltpu.VMEM((2, depth, 2 * n), BF16),
            pltpu.VMEM((half, n), F32),
            pltpu.VMEM((zs, half, 2 * n), F32),
            pltpu.VMEM((zs, half, 2 * n), F32),
            pltpu.VMEM((zs, half, 2 * n), F32),
            pltpu.VMEM((zs - 1, half, 2 * n), F32),
            pltpu.VMEM((zs - 1, half, 2 * n), F32),
            pltpu.VMEM((chunk, 2 * n), F32),
            pltpu.VMEM((outs, 8, half), F32),
            pltpu.VMEM((8, half), F32),
            pltpu.VMEM((zs, chunk, 2 * n), BF16),
            DMA((zs,)), DMA((4,)),
            DMA((zs,)), DMA((zs,)),
            DMA((zs - 1, 2)), DMA((zs - 1, 2)),
            DMA((outs,)), DMA((outs,)),
            DMA((len(TREE),)), DMA((len(TREE),)),
            DMA((zs,)), DMA((zs,)),
        ],
        compiler_params=pltpu.CompilerParams(
            collective_id=0, has_side_effects=True, vmem_limit_bytes=24 * 1024 * 1024
        ),
    )(*operands)
    return pl.pallas_call(
        finish,
        out_shape=(jax.ShapeDtypeStruct((depth, n), F32),) * 2,
        in_specs=[near] * 3,
        out_specs=(anywhere,) * 2,
        scratch_shapes=[pltpu.VMEM((depth, n), F32)] * 2 + [DMA((PIECES, 2))],
        compiler_params=pltpu.CompilerParams(vmem_limit_bytes=24 * 1024 * 1024),
    )(*(pltpu.with_memory_space_constraint(v, pltpu.VMEM) for v in (acc, pt, w)))


def solution(mesh):
    in_specs = (P(None, "inp"), P("inp", "out"), P("inp", "out"), P(None, "out"))
    out_specs = (P("inp", "out"), P("inp", "out"))
    fn = functools.partial(body, mesh.shape["inp"] // 2, mesh.shape["out"])
    return jax.shard_map(fn, mesh=mesh, in_specs=in_specs, out_specs=out_specs, check_vma=False)
```

```python
import functools

import jax
import jax.numpy as jnp
from jax import lax
from jax.experimental import pallas as pl
from jax.experimental.pallas import tpu as pltpu
from jax.sharding import PartitionSpec as P

P_SIZE = 1024
MESH = pl.DeviceIdType.MESH
TREE = ((0, 2), (0, -2), (0, 1), (0, -1), (2, 4), (2, 3), (-2, -3))
LATE = 3
PIECES = 8
JOIN = (5, 6)
PARTS = 2
SUBS = 2
F32 = jnp.float32
BF16 = jnp.bfloat16
SIN = (7.07104388e-01, -2.94595328e-02, 3.67091170e-04, -2.02891555e-06)
COS = (1.41420408e00, -1.76745738e-01, 3.66703335e-03, -2.80900148e-05)


def cos_sin(x):
    u = x * x
    s = x * (SIN[0] + u * (SIN[1] + u * (SIN[2] + u * SIN[3])))
    c = COS[0] + u * (COS[1] + u * (COS[2] + u * COS[3]))
    return 1.0 - s * s, s * c


def twice(w, n):
    return jnp.concatenate([w, jnp.concatenate([w[:, n:], -w[:, :n]], axis=1)], axis=0)


def front(
    zs, outs, ph_hbm, tr_hbm, ti_hbm, me_hbm, acc, pt, w_late,
    ph, rhs, meas, part, give, sib, ring, send, ring16, send16, field, pw, pws, w,
    in_sem, t_sem, sib_s, sib_r, far_s, far_r, ring_s, ring_r, pw_s, pw_r, ag_s, ag_r, agb_s, agb_r,
):
    chunk, half, n = ph.shape[1], ph.shape[1] // 2, meas.shape[1]
    depth, slab = ph.shape[2], min(256, ph.shape[2])
    sub = half // SUBS
    me = lax.axis_index("inp")
    peer = lax.axis_index("out")
    z, core = me // 2, me % 2
    step = 1 - 2 * core

    def at(d):
        return lax.rem(z + step * d + zs, zs) * 2 + core

    other = z * 2 + 1 - core
    up, down = lax.rem(z + 1, zs) * 2 + core, lax.rem(z + zs - 1, zs) * 2 + core
    mine = pl.multiple_of(core * half, half)
    theirs = pl.multiple_of((1 - core) * half, half)

    def chunk_of(i):
        off = jnp.where(i % 2 == 1, 4 - (i + 1) // 2, i // 2 - 4)
        return lax.rem(z + off + zs, zs)

    def load_phase(i):
        rows = pl.ds(pl.multiple_of(chunk_of(i) * chunk, chunk), chunk)
        return pltpu.make_async_copy(ph_hbm.at[rows], ph.at[i], in_sem.at[i])

    loads = []
    for j in range(PARTS):
        rows = pl.ds(j * (depth // PARTS), depth // PARTS)
        loads.append(
            [
                pltpu.make_async_copy(
                    source.at[rows], rhs.at[0, rows, pl.ds(k * n, n)], t_sem.at[j, k]
                )
                for k, source in enumerate((tr_hbm, ti_hbm))
            ]
        )
    load_phase(0).start()
    for pair in loads:
        for copy in pair:
            copy.start()
    for i in range(1, zs):
        load_phase(i).start()
    own_rows = pl.ds(pl.multiple_of(z * chunk + core * half, half), half)
    load_meas = pltpu.make_async_copy(me_hbm.at[own_rows], meas, t_sem.at[PARTS, 0])
    load_meas.start()

    barrier = pltpu.get_barrier_semaphore()
    for target in (other, up, down, at(2), at(-2)):
        pl.semaphore_signal(barrier, inc=1, device_id={"inp": target}, device_id_type=MESH)
    for j in range(1, outs):
        pl.semaphore_signal(
            barrier, inc=1, device_id={"out": lax.rem(peer + j, outs)}, device_id_type=MESH
        )

    def to_sibling(i):
        return pltpu.make_async_remote_copy(
            src_ref=give.at[i], dst_ref=sib.at[i], send_sem=sib_s.at[i], recv_sem=sib_r.at[i],
            device_id={"inp": other}, device_id_type=MESH,
        )

    def hop16(i):
        target = jnp.where(i == 0, at(2), jnp.where(i == 1, up, down))
        return pltpu.make_async_remote_copy(
            src_ref=send16.at[i], dst_ref=ring16.at[i],
            send_sem=far_s.at[i], recv_sem=far_r.at[i],
            device_id={"inp": target}, device_id_type=MESH,
        )

    def hop32(i, h):
        rows = pl.ds(h * sub, sub)
        return pltpu.make_async_remote_copy(
            src_ref=send.at[i - 3, rows], dst_ref=ring.at[i - 3, rows],
            send_sem=ring_s.at[i - 3, h], recv_sem=ring_r.at[i - 3, h],
            device_id={"inp": up if i % 2 == 1 else down}, device_id_type=MESH,
        )

    def forward(i, first=False):
        load_phase(i).wait()
        total = None
        for j in range(depth // slab):
            cols = slice(j * slab, (j + 1) * slab)
            if first and j % (depth // slab // PARTS) == 0:
                part_no = j // (depth // slab // PARTS)
                for copy in loads[part_no]:
                    copy.wait()
                rows = slice(part_no * (depth // PARTS), (part_no + 1) * (depth // PARTS))
                rhs[1, rows, 0:n] = -rhs[0, rows, n:]
                rhs[1, rows, n:] = rhs[0, rows, 0:n]
            re, im = cos_sin(ph[i, :, cols].astype(F32))
            re, im = re.astype(BF16), im.astype(BF16)
            pt[i, cols, 0:chunk] = re.T
            pt[i, cols, chunk:] = im.T
            left = jnp.concatenate([re, im], axis=1)
            right = jnp.concatenate([rhs[0, cols, :], rhs[1, cols, :]], axis=0)
            term = jnp.dot(left, right, preferred_element_type=F32)
            total = term if total is None else total + term
        field[...] = total
        part[i] = field[pl.ds(mine, half), :]
        give[i] = field[pl.ds(theirs, half), :]

    def pass_single(i):
        to_sibling(i).wait_recv()
        send16[i] = (part[i] + sib[i]).astype(BF16)
        hop16(i).start()

    def pass_joint(i):
        to_sibling(i).wait_recv()
        hop16(i - 2).wait_recv()

        @pl.when(core == i - 3)
        def _():
            hop16(0).wait_recv()

        for h in range(SUBS):
            rows = slice(h * sub, (h + 1) * sub)
            value = part[i, rows, :] + sib[i, rows, :] + ring16[i - 2, rows, :].astype(F32)

            @pl.when(core == i - 3)
            def _():
                send[i - 3, rows, :] = value + ring16[0, rows, :].astype(F32)

            @pl.when(core != i - 3)
            def _():
                send[i - 3, rows, :] = value

            hop32(i, h).start()

    def pass_last(i, h):
        rows = slice(h * sub, (h + 1) * sub)
        value = part[i, rows, :] + sib[i, rows, :]
        hop32(i - 2, h).wait_recv()
        send[i - 3, rows, :] = value + ring[i - 5, rows, :]
        hop32(i, h).start()

    forward(0, True)
    pl.semaphore_wait(barrier, 5 + outs - 1)
    to_sibling(0).start()

    def body(i, _):
        forward(i)
        to_sibling(i).start()

        @pl.when(i < 4)
        def _():
            pass_single(i - 1)

        @pl.when(i == JOIN[0])
        def _():
            pass_joint(3)

        @pl.when(i == JOIN[1])
        def _():
            pass_joint(4)

        return 0

    lax.fori_loop(1, zs, body, 0)
    for i in (5, 6):
        to_sibling(i).wait_recv()
    for i in (5, 6):
        for h in range(SUBS):
            pass_last(i, h)

    def lane_sum(v):
        folded = v[:, 0:128]
        for k in range(1, n // 128):
            folded = folded + v[:, k * 128 : (k + 1) * 128]
        return jnp.sum(folded.T, axis=0, keepdims=True)

    load_meas.wait()
    light = meas[...]
    light_sum = lane_sum(light)
    to_sibling(zs - 1).wait_recv()
    total = part[zs - 1] + sib[zs - 1]
    for i in (5, 6):
        for h in range(SUBS):
            hop32(i, h).wait_recv()
        total = total + ring[i - 3]
    f_re, f_im = total[:, :n], total[:, n:]
    power = f_re * f_re + f_im * f_im
    pws[:, 0:half] = lane_sum(power)
    pws[:, half:] = light_sum

    def to_peer(j):
        return pltpu.make_async_remote_copy(
            src_ref=pws, dst_ref=pw.at[j], send_sem=pw_s.at[j], recv_sem=pw_r.at[j],
            device_id={"out": lax.rem(peer + j, outs)}, device_id_type=MESH,
        )

    for j in range(1, outs):
        to_peer(j).start()
    sums = pws[...]
    for j in range(1, outs):
        to_peer(j).wait_recv()
        sums = sums + pw[j]
    scale = sums[:, half:] / (sums[:, 0:half] + 1e-05)
    scale = jnp.broadcast_to(scale, (128, half)).T
    scale = jnp.concatenate([scale] * (n // 128), axis=1)
    factor = scale * (scale * power - light)
    own = pl.ds(mine, half)
    w[zs - 1, own, 0:n] = (factor * f_re).astype(BF16)
    w[zs - 1, own, n:] = (factor * f_im).astype(BF16)

    def slot_of(d):
        if d == 0:
            return zs - 1
        if d == 4:
            return 0
        return 8 - 2 * d - core if d > 0 else 7 + 2 * d + core

    def pass_on(k, h):
        d, there = TREE[k]
        rows = pl.ds(pl.multiple_of(mine + h * sub, sub), sub)
        return pltpu.make_async_remote_copy(
            src_ref=w.at[slot_of(d), rows], dst_ref=w.at[slot_of(there), rows],
            send_sem=ag_s.at[k, h], recv_sem=ag_r.at[k, h],
            device_id={"inp": at(there - d)}, device_id_type=MESH,
        )

    def share(slot, h, rows0):
        rows = pl.ds(pl.multiple_of(rows0 + h * sub, sub), sub)
        return pltpu.make_async_remote_copy(
            src_ref=w.at[slot, rows], dst_ref=w.at[slot, rows],
            send_sem=agb_s.at[slot, h], recv_sem=agb_r.at[slot, h],
            device_id={"inp": other}, device_id_type=MESH,
        )

    def arrive(group):
        for h in range(SUBS):
            for k in group:
                pass_on(k, h).wait_recv()
                for later in range(len(TREE)):
                    if TREE[later][0] == TREE[k][1]:
                        pass_on(later, h).start()
                share(slot_of(TREE[k][1]), h, mine).start()

    block = min(512, depth)

    def backward(slots, first):
        for s in slots:
            for h in range(SUBS):
                share(s, h, theirs).wait_recv()

        def rows_of(b, _):
            rows = pl.ds(pl.multiple_of(b * block, block), block)
            value = None
            for s in slots:
                term = jnp.dot(pt[s, rows, :], twice(w[s], n), preferred_element_type=F32)
                value = term if value is None else value + term
            if not first:
                value = value + acc[rows, :]
            acc[rows, :] = value
            return 0

        lax.fori_loop(0, depth // block, rows_of, 0)

    for group in ((0, 1), (2, 3)):
        for h in range(SUBS):
            for k in group:
                pass_on(k, h).start()
    for h in range(SUBS):
        share(zs - 1, h, mine).start()
    backward((zs - 1,), True)
    arrive((0, 1))
    arrive((2, 3))
    backward((3, 4, 5, 6), False)

    def drain(i, _):
        to_sibling(i).wait_send()
        return 0

    lax.fori_loop(0, zs, drain, 0)
    for i in range(3):
        hop16(i).wait_send()
    for i in range(3, 7):
        for h in range(SUBS):
            hop32(i, h).wait_send()
    for j in range(1, outs):
        to_peer(j).wait_send()
    for k in range(4):
        for h in range(SUBS):
            pass_on(k, h).wait_send()

    arrive((4, 5, 6))
    for s in range(LATE):
        for h in range(SUBS):
            share(s, h, theirs).wait_recv()
        w_late[s] = w[s]
    for k in range(4, len(TREE)):
        for h in range(SUBS):
            pass_on(k, h).wait_send()
    for s in range(zs):
        for h in range(SUBS):
            share(s, h, mine).wait_send()


def finish(acc, pt, w, re_hbm, im_hbm, re, im, sem):
    n, depth = re.shape[1], re.shape[0]
    block = depth // PIECES
    norm = 1.0 / float(P_SIZE) ** 0.5
    copies = []
    for b in range(PIECES):
        rows = slice(b * block, (b + 1) * block)
        value = acc[rows, :]
        for s in range(LATE):
            value = value + jnp.dot(pt[s, rows, :], twice(w[s], n), preferred_element_type=F32)
        re[rows, :] = value[:, :n] * norm
        im[rows, :] = value[:, n:] * norm
        for i, (here, there) in enumerate(((re, re_hbm), (im, im_hbm))):
            there = there.at[pl.ds(b * block, block)]
            copies.append(pltpu.make_async_copy(here.at[pl.ds(b * block, block)], there, sem.at[b, i]))
            copies[-1].start()
    for copy in copies:
        copy.wait()


def body(zs, outs, phases, transfer_re, transfer_im, measured):
    probes, depth = phases.shape
    n = transfer_re.shape[1]
    chunk = probes // zs
    half = chunk // 2
    DMA = pltpu.SemaphoreType.DMA
    anywhere = pl.BlockSpec(memory_space=pl.ANY)
    near = pl.BlockSpec(memory_space=pltpu.VMEM)
    operands = [
        pltpu.with_memory_space_constraint(v, pltpu.HBM)
        for v in (phases, transfer_re, transfer_im, measured)
    ]
    acc, pt, w = pl.pallas_call(
        functools.partial(front, zs, outs),
        out_shape=(
            pltpu.VMEM((depth, 2 * n), F32),
            pltpu.VMEM((zs, depth, 2 * chunk), BF16),
            pltpu.VMEM((LATE, chunk, 2 * n), BF16),
        ),
        in_specs=[pl.BlockSpec(memory_space=pltpu.HBM)] * 4,
        out_specs=(near,) * 3,
        scratch_shapes=[
            pltpu.VMEM((zs, chunk, depth), BF16),
            pltpu.VMEM((2, depth, 2 * n), BF16),
            pltpu.VMEM((half, n), F32),
            pltpu.VMEM((zs, half, 2 * n), F32),
            pltpu.VMEM((zs, half, 2 * n), F32),
            pltpu.VMEM((zs, half, 2 * n), F32),
            pltpu.VMEM((4, half, 2 * n), F32),
            pltpu.VMEM((4, half, 2 * n), F32),
            pltpu.VMEM((3, half, 2 * n), BF16),
            pltpu.VMEM((3, half, 2 * n), BF16),
            pltpu.VMEM((chunk, 2 * n), F32),
            pltpu.VMEM((outs, 1, 2 * half), F32),
            pltpu.VMEM((1, 2 * half), F32),
            pltpu.VMEM((zs, chunk, 2 * n), BF16),
            DMA((zs,)), DMA((PARTS + 1, 2)),
            DMA((zs,)), DMA((zs,)),
            DMA((3,)), DMA((3,)), DMA((4, SUBS)), DMA((4, SUBS)),
            DMA((outs,)), DMA((outs,)),
            DMA((len(TREE), SUBS)), DMA((len(TREE), SUBS)),
            DMA((zs, SUBS)), DMA((zs, SUBS)),
        ],
        compiler_params=pltpu.CompilerParams(
            collective_id=0, has_side_effects=True, vmem_limit_bytes=24 * 1024 * 1024
        ),
    )(*operands)
    return pl.pallas_call(
        finish,
        out_shape=(jax.ShapeDtypeStruct((depth, n), F32),) * 2,
        in_specs=[near] * 3,
        out_specs=(anywhere,) * 2,
        scratch_shapes=[pltpu.VMEM((depth, n), F32)] * 2 + [DMA((PIECES, 2))],
        compiler_params=pltpu.CompilerParams(vmem_limit_bytes=24 * 1024 * 1024),
    )(*(pltpu.with_memory_space_constraint(v, pltpu.VMEM) for v in (acc, pt, w)))


def solution(mesh):
    in_specs = (P(None, "inp"), P("inp", "out"), P("inp", "out"), P(None, "out"))
    out_specs = (P("inp", "out"), P("inp", "out"))
    fn = functools.partial(body, mesh.shape["inp"] // 2, mesh.shape["out"])
    return jax.shard_map(fn, mesh=mesh, in_specs=in_specs, out_specs=out_specs, check_vma=False)
```

```python
import functools

import jax
import jax.numpy as jnp
from jax import lax
from jax.experimental import pallas as pl
from jax.experimental.pallas import tpu as pltpu
from jax.sharding import PartitionSpec as P

P_SIZE = 1024
MESH = pl.DeviceIdType.MESH
TREE = ((0, 2), (0, -2), (0, 1), (0, -1), (2, 4), (2, 3), (-2, -3))
LATE = 3
PIECES = 8
JOIN = (5, 6)
PARTS = 4
HOPS = 4
SUBS = 2
F32 = jnp.float32
BF16 = jnp.bfloat16
SIN = (7.07104388e-01, -2.94595328e-02, 3.67091170e-04, -2.02891555e-06)
COS = (1.41420408e00, -1.76745738e-01, 3.66703335e-03, -2.80900148e-05)


def cos_sin(x):
    u = x * x
    s = x * (SIN[0] + u * (SIN[1] + u * (SIN[2] + u * SIN[3])))
    c = COS[0] + u * (COS[1] + u * (COS[2] + u * COS[3]))
    return 1.0 - s * s, s * c


def twice(w, n):
    return jnp.concatenate([w, jnp.concatenate([w[:, n:], -w[:, :n]], axis=1)], axis=0)


def front(
    zs, outs, ph_hbm, tr_hbm, ti_hbm, me_hbm, acc, pt, w_late,
    ph, rhs, meas, part, give, sib, ring, send, ring16, send16, field, pw, pws, w,
    in_sem, t_sem, sib_s, sib_r, far_s, far_r, ring_s, ring_r, pw_s, pw_r, ag_s, ag_r, agb_s, agb_r,
):
    chunk, half, n = ph.shape[1], ph.shape[1] // 2, meas.shape[1]
    depth, slab = ph.shape[2], min(256, ph.shape[2])
    sub = half // SUBS
    me = lax.axis_index("inp")
    peer = lax.axis_index("out")
    z, core = me // 2, me % 2
    step = 1 - 2 * core

    def at(d):
        return lax.rem(z + step * d + zs, zs) * 2 + core

    other = z * 2 + 1 - core
    up, down = lax.rem(z + 1, zs) * 2 + core, lax.rem(z + zs - 1, zs) * 2 + core
    mine = pl.multiple_of(core * half, half)
    theirs = pl.multiple_of((1 - core) * half, half)

    def chunk_of(i):
        off = jnp.where(i % 2 == 1, 4 - (i + 1) // 2, i // 2 - 4)
        return lax.rem(z + off + zs, zs)

    def load_phase(i):
        rows = pl.ds(pl.multiple_of(chunk_of(i) * chunk, chunk), chunk)
        return pltpu.make_async_copy(ph_hbm.at[rows], ph.at[i], in_sem.at[i])

    loads = []
    for j in range(PARTS):
        rows = pl.ds(j * (depth // PARTS), depth // PARTS)
        loads.append(
            [
                pltpu.make_async_copy(
                    source.at[rows], rhs.at[0, rows, pl.ds(k * n, n)], t_sem.at[j, k]
                )
                for k, source in enumerate((tr_hbm, ti_hbm))
            ]
        )
    load_phase(0).start()
    for pair in loads:
        for copy in pair:
            copy.start()
    for i in range(1, zs):
        load_phase(i).start()
    own_rows = pl.ds(pl.multiple_of(z * chunk + core * half, half), half)
    load_meas = pltpu.make_async_copy(me_hbm.at[own_rows], meas, t_sem.at[PARTS, 0])
    load_meas.start()

    barrier = pltpu.get_barrier_semaphore()
    for target in (other, up, down, at(2), at(-2)):
        pl.semaphore_signal(barrier, inc=1, device_id={"inp": target}, device_id_type=MESH)
    for j in range(1, outs):
        pl.semaphore_signal(
            barrier, inc=1, device_id={"out": lax.rem(peer + j, outs)}, device_id_type=MESH
        )

    def to_sibling(i):
        return pltpu.make_async_remote_copy(
            src_ref=give.at[i], dst_ref=sib.at[i], send_sem=sib_s.at[i], recv_sem=sib_r.at[i],
            device_id={"inp": other}, device_id_type=MESH,
        )

    def hop16(i):
        target = jnp.where(i == 0, at(2), jnp.where(i == 1, up, down))
        return pltpu.make_async_remote_copy(
            src_ref=send16.at[i], dst_ref=ring16.at[i],
            send_sem=far_s.at[i], recv_sem=far_r.at[i],
            device_id={"inp": target}, device_id_type=MESH,
        )

    def hop32(i, h):
        rows = pl.ds(h * (half // HOPS), half // HOPS)
        return pltpu.make_async_remote_copy(
            src_ref=send.at[i - 3, rows], dst_ref=ring.at[i - 3, rows],
            send_sem=ring_s.at[i - 3, h], recv_sem=ring_r.at[i - 3, h],
            device_id={"inp": up if i % 2 == 1 else down}, device_id_type=MESH,
        )

    def forward(i, first=False):
        load_phase(i).wait()
        total = None
        for j in range(depth // slab):
            cols = slice(j * slab, (j + 1) * slab)
            if first and j % (depth // slab // PARTS) == 0:
                part_no = j // (depth // slab // PARTS)
                for copy in loads[part_no]:
                    copy.wait()
                rows = slice(part_no * (depth // PARTS), (part_no + 1) * (depth // PARTS))
                rhs[1, rows, 0:n] = -rhs[0, rows, n:]
                rhs[1, rows, n:] = rhs[0, rows, 0:n]
            re, im = cos_sin(ph[i, :, cols].astype(F32))
            re, im = re.astype(BF16), im.astype(BF16)
            pt[i, cols, 0:chunk] = re.T
            pt[i, cols, chunk:] = im.T
            left = jnp.concatenate([re, im], axis=1)
            right = jnp.concatenate([rhs[0, cols, :], rhs[1, cols, :]], axis=0)
            term = jnp.dot(left, right, preferred_element_type=F32)
            total = term if total is None else total + term
        field[...] = total
        part[i] = field[pl.ds(mine, half), :]
        give[i] = field[pl.ds(theirs, half), :]

    def pass_single(i):
        to_sibling(i).wait_recv()
        send16[i] = (part[i] + sib[i]).astype(BF16)
        hop16(i).start()

    def pass_joint(i):
        to_sibling(i).wait_recv()
        hop16(i - 2).wait_recv()

        @pl.when(core == i - 3)
        def _():
            hop16(0).wait_recv()

        for h in range(HOPS):
            rows = slice(h * (half // HOPS), (h + 1) * (half // HOPS))
            value = part[i, rows, :] + sib[i, rows, :] + ring16[i - 2, rows, :].astype(F32)

            @pl.when(core == i - 3)
            def _():
                send[i - 3, rows, :] = value + ring16[0, rows, :].astype(F32)

            @pl.when(core != i - 3)
            def _():
                send[i - 3, rows, :] = value

            hop32(i, h).start()

    def pass_last(i, h):
        rows = slice(h * (half // HOPS), (h + 1) * (half // HOPS))
        value = part[i, rows, :] + sib[i, rows, :]
        hop32(i - 2, h).wait_recv()
        send[i - 3, rows, :] = value + ring[i - 5, rows, :]
        hop32(i, h).start()

    forward(0, True)
    pl.semaphore_wait(barrier, 5 + outs - 1)
    to_sibling(0).start()

    def body(i, _):
        forward(i)
        to_sibling(i).start()

        @pl.when(i < 4)
        def _():
            pass_single(i - 1)

        @pl.when(i == JOIN[0])
        def _():
            pass_joint(3)

        @pl.when(i == JOIN[1])
        def _():
            pass_joint(4)

        return 0

    lax.fori_loop(1, zs, body, 0)
    for i in (5, 6):
        to_sibling(i).wait_recv()
    for h in range(HOPS):
        for i in (5, 6):
            pass_last(i, h)

    def lane_sum(v):
        folded = v[:, 0:128]
        for k in range(1, n // 128):
            folded = folded + v[:, k * 128 : (k + 1) * 128]
        return jnp.sum(folded.T, axis=0, keepdims=True)

    load_meas.wait()
    light = meas[...]
    light_sum = lane_sum(light)
    to_sibling(zs - 1).wait_recv()
    total = part[zs - 1] + sib[zs - 1]
    for i in (5, 6):
        for h in range(HOPS):
            hop32(i, h).wait_recv()
        total = total + ring[i - 3]
    f_re, f_im = total[:, :n], total[:, n:]
    power = f_re * f_re + f_im * f_im
    pws[:, 0:half] = lane_sum(power)
    pws[:, half:] = light_sum

    def to_peer(j):
        return pltpu.make_async_remote_copy(
            src_ref=pws, dst_ref=pw.at[j], send_sem=pw_s.at[j], recv_sem=pw_r.at[j],
            device_id={"out": lax.rem(peer + j, outs)}, device_id_type=MESH,
        )

    for j in range(1, outs):
        to_peer(j).start()
    sums = pws[...]
    for j in range(1, outs):
        to_peer(j).wait_recv()
        sums = sums + pw[j]
    scale = sums[:, half:] / (sums[:, 0:half] + 1e-05)
    scale = jnp.broadcast_to(scale, (128, half)).T
    scale = jnp.concatenate([scale] * (n // 128), axis=1)
    factor = scale * (scale * power - light)
    own = pl.ds(mine, half)
    w[zs - 1, own, 0:n] = (factor * f_re).astype(BF16)
    w[zs - 1, own, n:] = (factor * f_im).astype(BF16)

    def slot_of(d):
        if d == 0:
            return zs - 1
        if d == 4:
            return 0
        return 8 - 2 * d - core if d > 0 else 7 + 2 * d + core

    def pass_on(k, h):
        d, there = TREE[k]
        rows = pl.ds(pl.multiple_of(mine + h * sub, sub), sub)
        return pltpu.make_async_remote_copy(
            src_ref=w.at[slot_of(d), rows], dst_ref=w.at[slot_of(there), rows],
            send_sem=ag_s.at[k, h], recv_sem=ag_r.at[k, h],
            device_id={"inp": at(there - d)}, device_id_type=MESH,
        )

    def share(slot, h, rows0):
        rows = pl.ds(pl.multiple_of(rows0 + h * sub, sub), sub)
        return pltpu.make_async_remote_copy(
            src_ref=w.at[slot, rows], dst_ref=w.at[slot, rows],
            send_sem=agb_s.at[slot, h], recv_sem=agb_r.at[slot, h],
            device_id={"inp": other}, device_id_type=MESH,
        )

    def arrive(group):
        for h in range(SUBS):
            for k in group:
                pass_on(k, h).wait_recv()
                for later in range(len(TREE)):
                    if TREE[later][0] == TREE[k][1]:
                        pass_on(later, h).start()
                share(slot_of(TREE[k][1]), h, mine).start()

    block = min(256, depth)

    def backward(slots, first):
        for s in slots:
            for h in range(SUBS):
                share(s, h, theirs).wait_recv()

        for b in range(depth // block):
            rows = slice(b * block, (b + 1) * block)
            value = None if first else acc[rows, :]
            for s in slots:
                term = jnp.dot(pt[s, rows, :], twice(w[s], n), preferred_element_type=F32)
                value = term if value is None else value + term
            acc[rows, :] = value

    for group in ((0, 1), (2, 3)):
        for h in range(SUBS):
            for k in group:
                pass_on(k, h).start()
    for h in range(SUBS):
        share(zs - 1, h, mine).start()
    backward((zs - 1,), True)
    arrive((0, 1))
    arrive((2, 3))
    backward((3, 4, 5, 6), False)

    def drain(i, _):
        to_sibling(i).wait_send()
        return 0

    lax.fori_loop(0, zs, drain, 0)
    for i in range(3):
        hop16(i).wait_send()
    for i in range(3, 7):
        for h in range(HOPS):
            hop32(i, h).wait_send()
    for j in range(1, outs):
        to_peer(j).wait_send()
    for k in range(4):
        for h in range(SUBS):
            pass_on(k, h).wait_send()

    arrive((4, 5, 6))
    for s in range(LATE):
        for h in range(SUBS):
            share(s, h, theirs).wait_recv()
        w_late[s] = w[s]
    for k in range(4, len(TREE)):
        for h in range(SUBS):
            pass_on(k, h).wait_send()
    for s in range(zs):
        for h in range(SUBS):
            share(s, h, mine).wait_send()


def finish(acc, pt, w, re_hbm, im_hbm, re, im, sem):
    n, depth = re.shape[1], re.shape[0]
    block = depth // PIECES
    norm = 1.0 / float(P_SIZE) ** 0.5
    copies = []
    for b in range(PIECES):
        rows = slice(b * block, (b + 1) * block)
        value = acc[rows, :]
        for s in range(LATE):
            value = value + jnp.dot(pt[s, rows, :], twice(w[s], n), preferred_element_type=F32)
        re[rows, :] = value[:, :n] * norm
        im[rows, :] = value[:, n:] * norm
        for i, (here, there) in enumerate(((re, re_hbm), (im, im_hbm))):
            there = there.at[pl.ds(b * block, block)]
            copies.append(pltpu.make_async_copy(here.at[pl.ds(b * block, block)], there, sem.at[b, i]))
            copies[-1].start()
    for copy in copies:
        copy.wait()


def body(zs, outs, phases, transfer_re, transfer_im, measured):
    probes, depth = phases.shape
    n = transfer_re.shape[1]
    chunk = probes // zs
    half = chunk // 2
    DMA = pltpu.SemaphoreType.DMA
    anywhere = pl.BlockSpec(memory_space=pl.ANY)
    near = pl.BlockSpec(memory_space=pltpu.VMEM)
    operands = [
        pltpu.with_memory_space_constraint(v, pltpu.HBM)
        for v in (phases, transfer_re, transfer_im, measured)
    ]
    acc, pt, w = pl.pallas_call(
        functools.partial(front, zs, outs),
        out_shape=(
            pltpu.VMEM((depth, 2 * n), F32),
            pltpu.VMEM((zs, depth, 2 * chunk), BF16),
            pltpu.VMEM((LATE, chunk, 2 * n), BF16),
        ),
        in_specs=[pl.BlockSpec(memory_space=pltpu.HBM)] * 4,
        out_specs=(near,) * 3,
        scratch_shapes=[
            pltpu.VMEM((zs, chunk, depth), BF16),
            pltpu.VMEM((2, depth, 2 * n), BF16),
            pltpu.VMEM((half, n), F32),
            pltpu.VMEM((zs, half, 2 * n), F32),
            pltpu.VMEM((zs, half, 2 * n), F32),
            pltpu.VMEM((zs, half, 2 * n), F32),
            pltpu.VMEM((4, half, 2 * n), F32),
            pltpu.VMEM((4, half, 2 * n), F32),
            pltpu.VMEM((3, half, 2 * n), BF16),
            pltpu.VMEM((3, half, 2 * n), BF16),
            pltpu.VMEM((chunk, 2 * n), F32),
            pltpu.VMEM((outs, 1, 2 * half), F32),
            pltpu.VMEM((1, 2 * half), F32),
            pltpu.VMEM((zs, chunk, 2 * n), BF16),
            DMA((zs,)), DMA((PARTS + 1, 2)),
            DMA((zs,)), DMA((zs,)),
            DMA((3,)), DMA((3,)), DMA((4, HOPS)), DMA((4, HOPS)),
            DMA((outs,)), DMA((outs,)),
            DMA((len(TREE), SUBS)), DMA((len(TREE), SUBS)),
            DMA((zs, SUBS)), DMA((zs, SUBS)),
        ],
        compiler_params=pltpu.CompilerParams(
            collective_id=0, has_side_effects=True, vmem_limit_bytes=24 * 1024 * 1024
        ),
    )(*operands)
    return pl.pallas_call(
        finish,
        out_shape=(jax.ShapeDtypeStruct((depth, n), F32),) * 2,
        in_specs=[near] * 3,
        out_specs=(anywhere,) * 2,
        scratch_shapes=[pltpu.VMEM((depth, n), F32)] * 2 + [DMA((PIECES, 2))],
        compiler_params=pltpu.CompilerParams(vmem_limit_bytes=24 * 1024 * 1024),
    )(*(pltpu.with_memory_space_constraint(v, pltpu.VMEM) for v in (acc, pt, w)))


def solution(mesh):
    in_specs = (P(None, "inp"), P("inp", "out"), P("inp", "out"), P(None, "out"))
    out_specs = (P("inp", "out"), P("inp", "out"))
    fn = functools.partial(body, mesh.shape["inp"] // 2, mesh.shape["out"])
    return jax.shard_map(fn, mesh=mesh, in_specs=in_specs, out_specs=out_specs, check_vma=False)
```
